256 devices in a mesh: row: 8 (over z), col: 16 (over x_hi, y, core), depth: 2 (over x_lo).
Axes of the slice: x: 4 (x_hi: 2, x_lo: 2; x = x_hi * 2 + x_lo), y: 4, z: 8, core: 2. Of those that a mesh axis runs over, the one named last changes fastest.
Arguments:
- a_matrix: bfloat16 [8192, 8192], P('col', 'row'), may hold values from -6 to 6
- b_matrix: bfloat16 [8192, 14336], P('col', 'row'), may hold values from -0.0625 to 0.0625
Outputs:
- product: bfloat16 [8192, 14336], P('col', ('row', 'depth'))
The draws below stay inside these ranges and needn't reach their ends.
All inputs are finite; a program needn't handle non-finite values.
Results may differ from the reference program's by a relative error of at most 0.0052.
Values may be sent and summed in bfloat16 or wider, within the bound.
No kernel may reach another device: no remote copies, remote signals or barrier semaphores. Data moves between devices by JAX's collectives and lax.ppermute only.
A program may use at most 64 MiB of HBM per device.

```python
import jax
import jax.numpy as jnp
from jax import lax

K = 8192
N = 14336
M = 8192
LAYERS = 2
PIECE = 512


def block_scale(own_key, extent, pieces, least, high):
    factor_of = 1.0
    for position, parts in pieces:
        draws = jax.random.uniform(jax.random.fold_in(jax.random.fold_in(own_key, 6), position), (parts,), jnp.float32, least / len(pieces), high / len(pieces))
        factor_of = factor_of * jnp.repeat(jnp.exp(draws), extent[position] // parts).reshape((-1,) + (1,) * (len(extent) - 1 - position))
    return factor_of


def gaussian(key, shape, scale, most, shards=(), kind=jnp.bfloat16):
    factor_of = block_scale(key, shape, shards, -0.22, 0.18) if shards else 1.0
    values = jax.random.normal(key, shape, jnp.float32) * scale * factor_of
    return jnp.minimum(jnp.maximum(values, -most), most).astype(kind)


def setup_inputs(seed: int = 0) -> dict:
    key_of = jax.random.split(jax.random.key(seed), 3)
    a_matrix = gaussian(key_of[0], (M, K), 1.0, 6.0, ((0, 16), (1, 8)))
    b_matrix = gaussian(key_of[1], (K, N), K ** -0.5, 0.0625, ((0, 16), (1, 8)))
    return {"a_matrix": a_matrix, "b_matrix": b_matrix}


def reference(a_matrix, b_matrix):
    row_total = a_matrix.shape[0]
    col_total = b_matrix.shape[1]
    groups = a_matrix.shape[1] // (LAYERS * PIECE)
    left_view = a_matrix.reshape(row_total, groups, LAYERS, PIECE)
    right_view = b_matrix.reshape(groups, LAYERS, PIECE, col_total)
    summed = jnp.zeros((row_total, col_total), jnp.float32)
    for layer_index in range(LAYERS):
        left_part = left_view[:, :, layer_index, :].reshape(row_total, groups * PIECE)
        right_part = right_view[:, layer_index, :, :].reshape(groups * PIECE, col_total)
        partial_value = jnp.dot(left_part, right_part, preferred_element_type=jnp.float32).astype(jnp.bfloat16)
        partial_value = lax.optimization_barrier(partial_value)
        summed = summed + partial_value.astype(jnp.float32)
    return summed.astype(jnp.bfloat16)
```

```python
import jax
import jax.numpy as jnp
from jax import lax
from jax.sharding import PartitionSpec as P

AXES = ("row", "col", "depth")
Z, X, Y = 8, 2, 4


def moved(value, target):
    def number(z, x_hi, y, core, x_lo):
        return (((z * X + x_hi) * Y + y) * 2 + core) * 2 + x_lo

    pairs = [
        (number(z, x_hi, y, core, x_lo), number(*target(z, x_hi, y, core, x_lo)))
        for z in range(Z) for x_hi in range(X) for y in range(Y) for core in range(2) for x_lo in range(2)
    ]
    return lax.ppermute(value, AXES, pairs)


def z_up(z, x_hi, y, core, x_lo):
    return (z + 1) % Z, x_hi, y, core, x_lo


def z_down(z, x_hi, y, core, x_lo):
    return (z - 1) % Z, x_hi, y, core, x_lo


def y_up(z, x_hi, y, core, x_lo):
    return z, x_hi, (y + 1) % Y, core, x_lo


def y_down(z, x_hi, y, core, x_lo):
    return z, x_hi, (y - 1) % Y, core, x_lo


def x_side(z, x_hi, y, core, x_lo):
    return z, 1 - x_hi, y, core, 1 - x_lo


def x_pair(z, x_hi, y, core, x_lo):
    return z, x_hi, y, core, 1 - x_lo


def sibling(z, x_hi, y, core, x_lo):
    return z, x_hi, y, 1 - core, x_lo


def body(a_matrix, b_matrix):
    rows, width = a_matrix.shape
    depth, columns = b_matrix.shape
    half = depth // 2
    z = lax.axis_index("row")
    col = lax.axis_index("col")
    x_lo = lax.axis_index("depth")
    x_hi, y, core = col // (2 * Y), col // 2 % Y, col % 2
    part = x_hi ^ x_lo

    a_view = a_matrix.reshape(rows, 2, 2, half)
    a_mine = lax.dynamic_slice(a_view, (0, core, part, 0), (rows, 1, 1, half)).reshape(rows, half)
    a_other = lax.dynamic_slice(a_view, (0, 1 - core, part, 0), (rows, 1, 1, half)).reshape(rows, half)
    piece = jnp.concatenate([a_mine, a_other], 1)
    a_pieces = [(piece, 0)]
    up = down = piece
    for step in range(1, Z // 2 + 1):
        up = moved(up, z_up)
        a_pieces.append((up, -step))
        if step < Z // 2:
            down = moved(down, z_down)
            a_pieces.append((down, step))
    left = [jnp.zeros((rows, Z * half), a_matrix.dtype) for _ in range(2)]
    for value, offset in a_pieces:
        place = (z + offset) % Z
        for k in range(2):
            left[k] = lax.dynamic_update_slice(left[k], value[:, k * half:(k + 1) * half], (0, place * half))

    own = lax.dynamic_slice(b_matrix, (part * half, 0), (half, columns))
    nb = moved(own, x_side)
    own_up = moved(own, y_up)
    own_down = moved(own, y_down)
    far_a = moved(own_up[: half // 2], y_up)
    far_b = moved(own_down[half // 2:], y_down)
    nb_up = moved(nb, y_up)
    nb_down = moved(nb, y_down)
    nb_far_a = moved(far_a, x_side)
    nb_far_b = moved(far_b, x_side)
    b_pieces = [(own, 0, 0, 0), (nb, 1, 0, 0), (own_up, 0, -1, 0), (own_down, 0, 1, 0), (far_a, 0, 2, 0), (far_b, 0, 2, 1),
                (nb_up, 1, -1, 0), (nb_down, 1, 1, 0), (nb_far_a, 1, 2, 0), (nb_far_b, 1, 2, 1)]
    right = [jnp.zeros((Z * half, columns), b_matrix.dtype) for _ in range(2)]
    for value, side, dy, sub in b_pieces:
        place = ((x_hi + side) % 2 * Y + (y + dy) % Y) * half + sub * (half // 2)
        right[0] = lax.dynamic_update_slice(right[0], value, (place, 0))
        right[1] = lax.dynamic_update_slice(right[1], moved(value, sibling), (place, 0))

    total = jnp.dot(left[0], right[0], preferred_element_type=jnp.float32)
    total = total + jnp.dot(left[1], right[1], preferred_element_type=jnp.float32)
    share = columns // 2
    away = lax.dynamic_slice(total, (0, (1 - x_lo) * share), (rows, share)).astype(jnp.bfloat16)
    keep = lax.dynamic_slice(total, (0, x_lo * share), (rows, share))
    return (keep + moved(away, x_pair).astype(jnp.float32)).astype(jnp.bfloat16)


def solution(mesh):
    in_specs = (P("col", "row"), P("col", "row"))
    out_specs = P("col", ("row", "depth"))
    return jax.shard_map(body, mesh=mesh, in_specs=in_specs, out_specs=out_specs, check_vma=False)
```

```python
import functools

import jax
import jax.numpy as jnp
from jax import lax
from jax.experimental import pallas as pl
from jax.experimental.pallas import tpu as pltpu
from jax.sharding import PartitionSpec as P

AXES = ("row", "col", "depth")
Z, X, Y = 8, 2, 4
TILE = 256


def moved(value, target):
    def number(z, x_hi, y, core, x_lo):
        return (((z * X + x_hi) * Y + y) * 2 + core) * 2 + x_lo

    pairs = [
        (number(z, x_hi, y, core, x_lo), number(*target(z, x_hi, y, core, x_lo)))
        for z in range(Z)
        for x_hi in range(X)
        for y in range(Y)
        for core in range(2)
        for x_lo in range(2)
    ]
    return lax.ppermute(value, AXES, pairs)


def z_up(z, x_hi, y, core, x_lo):
    return (z + 1) % Z, x_hi, y, core, x_lo


def z_down(z, x_hi, y, core, x_lo):
    return (z - 1) % Z, x_hi, y, core, x_lo


def y_up(z, x_hi, y, core, x_lo):
    return z, x_hi, (y + 1) % Y, core, x_lo


def y_down(z, x_hi, y, core, x_lo):
    return z, x_hi, (y - 1) % Y, core, x_lo


def x_side(z, x_hi, y, core, x_lo):
    return z, 1 - x_hi, y, core, 1 - x_lo


def x_pair(z, x_hi, y, core, x_lo):
    return z, x_hi, y, core, 1 - x_lo


def sibling(z, x_hi, y, core, x_lo):
    return z, x_hi, y, 1 - core, x_lo


def pack_kernel(places, *refs):
    pieces, packed, sem = refs[:len(places)], refs[-2], refs[-1]
    rows = packed.shape[1] // 2
    z = lax.axis_index("row")
    copies = []
    for index, (block, offset) in enumerate(places):
        place = packed.at[lax.rem(z + offset, Z), pl.ds(block * rows, pieces[index].shape[0])]
        copies.append(pltpu.make_async_copy(pieces[index], place, sem.at[index]))
    for copy in copies:
        copy.start()
    for copy in copies:
        copy.wait()


def packed_left(pieces, rows):
    values, places = zip(*pieces)
    half = values[0].shape[1]
    return pl.pallas_call(
        functools.partial(pack_kernel, places),
        out_shape=jax.ShapeDtypeStruct((Z, 2 * rows, half), jnp.bfloat16),
        in_specs=[pl.BlockSpec(memory_space=pl.ANY)] * len(values),
        out_specs=pl.BlockSpec(memory_space=pltpu.VMEM),
        scratch_shapes=[pltpu.SemaphoreType.DMA((len(values),))],
        compiler_params=pltpu.CompilerParams(vmem_limit_bytes=12 * 1024 * 1024),
        cost_estimate=pl.CostEstimate(flops=0, bytes_accessed=8 * Z * rows * half, transcendentals=0),
    )(*values)


def product_kernel(places, left, *refs):
    rights = refs[:len(places)]
    keep, send, total = refs[len(places):]
    _, rows, share = keep.shape
    col = lax.axis_index("col")
    x_lo = lax.axis_index("depth")
    x_hi, y = col // (2 * Y), col // 2 % Y
    for block in (1, 0):
        for index, (side, dy, first) in enumerate(places):
            place = lax.rem(x_hi + side, X) * Y + lax.rem(y + dy, Y)
            term = jnp.dot(
                left[place, block * rows:(block + 1) * rows],
                rights[index][:, first:first + 2 * share],
                preferred_element_type=jnp.float32,
            )
            total[...] = total[...] + term if index else term
        for d in range(2):
            target = send if block else keep
            target[lax.rem(x_lo + d, 2)] = total[:, d * share:(d + 1) * share].astype(target.dtype)


def product(left, pieces, columns):
    values, places = zip(*pieces)
    rows, inner = left.shape[1] // 2, left.shape[0] * left.shape[2]
    vmem = pl.BlockSpec(memory_space=pltpu.VMEM)
    return pl.pallas_call(
        functools.partial(product_kernel, places),
        out_shape=(
            jax.ShapeDtypeStruct((2, rows, columns // 2), jnp.float32),
            jax.ShapeDtypeStruct((2, rows, columns // 2), jnp.bfloat16),
        ),
        in_specs=[vmem] * (1 + len(values)),
        out_specs=(vmem, vmem),
        scratch_shapes=[pltpu.VMEM((rows, columns), jnp.float32)],
        compiler_params=pltpu.CompilerParams(vmem_limit_bytes=24 * 1024 * 1024),
        cost_estimate=pl.CostEstimate(
            flops=4 * rows * inner * columns, bytes_accessed=4 * inner * (rows + columns), transcendentals=0
        ),
    )(left, *values)


class Held:
    def __init__(self, **values):
        self.values = dict(values)

    def gate(self, *names):
        names = list(dict.fromkeys(names))
        if len(names) > 1:
            for name, value in zip(names, lax.optimization_barrier([self.values[n] for n in names]), strict=True):
                self.values[name] = value

    def move(self, name, source, target, after=()):
        self.gate(source, *after)
        self.values[name] = moved(self.values[source], target)


def body(a_matrix, b_matrix):
    rows = a_matrix.shape[0]
    depth, columns = b_matrix.shape
    half = depth // 2
    share = columns // 2
    col = lax.axis_index("col")
    x_lo = lax.axis_index("depth")
    x_hi, core = col // (2 * Y), col % 2
    part = x_hi ^ x_lo
    wide = -(-share // (2 * TILE)) * TILE

    def cut(first, width):
        return jnp.concatenate(
            [lax.dynamic_slice(b_matrix, (part * half, d * share + first), (half, width)) for d in range(2)], 1
        )

    other = lax.dynamic_slice(a_matrix, (0, (1 - core) * depth + part * half), (rows, half))
    mine = lax.dynamic_slice(a_matrix, (0, core * depth + part * half), (rows, half))
    held = Held(o=jnp.concatenate([cut(0, wide), cut(wide, share - wide)], 1))
    values, move, gate = held.values, held.move, held.gate
    values["other"] = other
    move("sib", "other", sibling)
    gate("sib", "o")
    move("u", "o", y_up)
    move("d", "o", y_down)
    move("n", "o", x_side)
    values["p"] = jnp.concatenate([mine, values["sib"]], 0)
    move("u1", "p", z_up)
    move("d1", "p", z_down)

    gate("u1", "d1")
    move("u2", "u1", z_up)
    move("d2", "d1", z_down)

    gate("u", "d", "n")
    values["ua"], values["db"] = values["u"][:, :2 * wide], values["d"][:, 2 * wide:]
    move("fa", "ua", y_up)
    move("fb", "db", y_down)

    gate("u2", "d2", "u", "d", "n")
    move("u3", "u2", z_up)
    move("d3", "d2", z_down)

    gate("fa", "fb", "u2", "d2", "n")
    move("nu", "n", y_up)
    move("nd", "n", y_down)
    move("nfa", "fa", x_side)
    move("nfb", "fb", x_side)

    gate("u3", "d3")
    values["u3h"], values["d3h"] = values["u3"][:rows], values["d3"][rows:]
    move("u4", "u3h", z_up)
    move("d4", "d3h", z_down)

    a_pieces = [("p", 0, 0), ("u1", 0, Z - 1), ("d1", 0, 1), ("u2", 0, Z - 2), ("d2", 0, 2),
                ("u3", 0, Z - 3), ("d3", 0, 3), ("u4", 0, Z // 2), ("d4", 1, Z // 2)]
    gate("nfa", "u4")
    left = packed_left([(values[k], tuple(v)) for k, *v in a_pieces], rows)
    parts = []
    for chunk, first in (("b", 2 * wide), ("a", 0)):
        b_pieces = [("o", 0, 0, first), ("n", 1, 0, first), ("u", 0, Y - 1, first), ("d", 0, 1, first), ("f" + chunk, 0, 2, 0),
                    ("nu", 1, Y - 1, first), ("nd", 1, 1, first), ("nf" + chunk, 1, 2, 0)]
        keep, send = product(left, [(values[k], tuple(v)) for k, *v in b_pieces],
                             values["f" + chunk].shape[1])
        came = moved(send, sibling)
        left, _ = lax.optimization_barrier((left, send))
        away = (keep[1] + came[1].astype(jnp.float32)).astype(jnp.bfloat16)
        arrived = moved(away, x_pair)
        parts.append((keep[0] + came[0].astype(jnp.float32) + arrived.astype(jnp.float32)).astype(jnp.bfloat16))
    first = lax.pad(parts[0], jnp.zeros((), jnp.bfloat16), ((0, 0, 0), (wide, 0, 0)))
    return lax.dynamic_update_slice(first, parts[1], (0, 0))


def solution(mesh):
    in_specs = (P("col", "row"), P("col", "row"))
    out_specs = P("col", ("row", "depth"))
    return jax.shard_map(body, mesh=mesh, in_specs=in_specs, out_specs=out_specs, check_vma=False)
```

```python
import functools

import jax
import jax.numpy as jnp
from jax import lax
from jax.experimental import pallas as pl
from jax.experimental.pallas import tpu as pltpu
from jax.sharding import PartitionSpec as P

AXES = ("row", "col", "depth")
Z, X, Y = 8, 2, 4
TILE = 256


def moved(value, target):
    def number(z, x_hi, y, core, x_lo):
        return (((z * X + x_hi) * Y + y) * 2 + core) * 2 + x_lo

    pairs = [
        (number(z, x_hi, y, core, x_lo), number(*target(z, x_hi, y, core, x_lo)))
        for z in range(Z)
        for x_hi in range(X)
        for y in range(Y)
        for core in range(2)
        for x_lo in range(2)
    ]
    return lax.ppermute(value, AXES, pairs)


def z_up(z, x_hi, y, core, x_lo):
    return (z + 1) % Z, x_hi, y, core, x_lo


def z_down(z, x_hi, y, core, x_lo):
    return (z - 1) % Z, x_hi, y, core, x_lo


def y_up(z, x_hi, y, core, x_lo):
    return z, x_hi, (y + 1) % Y, core, x_lo


def y_down(z, x_hi, y, core, x_lo):
    return z, x_hi, (y - 1) % Y, core, x_lo


def x_side(z, x_hi, y, core, x_lo):
    return z, 1 - x_hi, y, core, 1 - x_lo


def x_pair(z, x_hi, y, core, x_lo):
    return z, x_hi, y, core, 1 - x_lo


def sibling(z, x_hi, y, core, x_lo):
    return z, x_hi, y, 1 - core, x_lo


def pack_kernel(places, *refs):
    pieces, packed, sem = refs[:len(places)], refs[-2], refs[-1]
    rows = packed.shape[1] // 2
    z = lax.axis_index("row")
    copies = []
    for index, (block, offset) in enumerate(places):
        place = packed.at[lax.rem(z + offset, Z), pl.ds(block * rows, pieces[index].shape[0])]
        copies.append(pltpu.make_async_copy(pieces[index], place, sem.at[index]))
    for copy in copies:
        copy.start()
    for copy in copies:
        copy.wait()


def packed_left(pieces, rows):
    values, places = zip(*pieces)
    half = values[0].shape[1]
    return pl.pallas_call(
        functools.partial(pack_kernel, places),
        out_shape=jax.ShapeDtypeStruct((Z, 2 * rows, half), jnp.bfloat16),
        in_specs=[pl.BlockSpec(memory_space=pl.ANY)] * len(values),
        out_specs=pl.BlockSpec(memory_space=pltpu.VMEM),
        scratch_shapes=[pltpu.SemaphoreType.DMA((len(values),))],
        compiler_params=pltpu.CompilerParams(vmem_limit_bytes=12 * 1024 * 1024),
        cost_estimate=pl.CostEstimate(flops=0, bytes_accessed=8 * Z * rows * half, transcendentals=0),
    )(*values)


def product_kernel(places, block, left, *refs):
    rights = refs[:len(places)]
    target, total = refs[len(places):]
    _, rows, share = target.shape
    col = lax.axis_index("col")
    x_lo = lax.axis_index("depth")
    x_hi, y = col // (2 * Y), col // 2 % Y
    for index, (side, dy, first) in enumerate(places):
        place = lax.rem(x_hi + side, X) * Y + lax.rem(y + dy, Y)
        term = jnp.dot(
            left[place, block * rows:(block + 1) * rows],
            rights[index][:, first:first + 2 * share],
            preferred_element_type=jnp.float32,
        )
        total[...] = total[...] + term if index else term
    for d in range(2):
        target[lax.rem(x_lo + d, 2)] = total[:, d * share:(d + 1) * share].astype(target.dtype)


def product(left, pieces, columns, block):
    values, places = zip(*pieces)
    rows, inner = left.shape[1] // 2, left.shape[0] * left.shape[2]
    vmem = pl.BlockSpec(memory_space=pltpu.VMEM)
    return pl.pallas_call(
        functools.partial(product_kernel, places, block),
        out_shape=jax.ShapeDtypeStruct((2, rows, columns // 2), jnp.bfloat16 if block else jnp.float32),
        in_specs=[vmem] * (1 + len(values)),
        out_specs=vmem,
        scratch_shapes=[pltpu.VMEM((rows, columns), jnp.float32)],
        compiler_params=pltpu.CompilerParams(vmem_limit_bytes=24 * 1024 * 1024),
        cost_estimate=pl.CostEstimate(
            flops=2 * rows * inner * columns, bytes_accessed=2 * inner * (rows + columns), transcendentals=0
        ),
    )(left, *values)


class Held:
    def __init__(self, **values):
        self.values = dict(values)

    def gate(self, *names):
        names = list(dict.fromkeys(names))
        if len(names) > 1:
            for name, value in zip(names, lax.optimization_barrier([self.values[n] for n in names]), strict=True):
                self.values[name] = value

    def move(self, name, source, target, after=()):
        self.gate(source, *after)
        self.values[name] = moved(self.values[source], target)


def body(a_matrix, b_matrix):
    rows = a_matrix.shape[0]
    depth, columns = b_matrix.shape
    half = depth // 2
    share = columns // 2
    col = lax.axis_index("col")
    x_lo = lax.axis_index("depth")
    x_hi, core = col // (2 * Y), col % 2
    part = x_hi ^ x_lo
    wide = -(-share // (2 * TILE)) * TILE

    def cut(first, width):
        return jnp.concatenate(
            [lax.dynamic_slice(b_matrix, (part * half, d * share + first), (half, width)) for d in range(2)], 1
        )

    other = lax.dynamic_slice(a_matrix, (0, (1 - core) * depth + part * half), (rows, half))
    mine = lax.dynamic_slice(a_matrix, (0, core * depth + part * half), (rows, half))
    held = Held(o=jnp.concatenate([cut(0, wide), cut(wide, share - wide)], 1))
    values, move, gate = held.values, held.move, held.gate
    values["other"] = other
    move("sib", "other", sibling)
    gate("sib", "o")
    move("u", "o", y_up)
    move("d", "o", y_down)
    move("n", "o", x_side)
    values["p"] = jnp.concatenate([mine, values["sib"]], 0)
    move("u1", "p", z_up)
    move("d1", "p", z_down)

    gate("u1", "d1")
    move("u2", "u1", z_up)
    move("d2", "d1", z_down)

    gate("u", "d", "n")
    values["ua"], values["db"] = values["u"][:, :2 * wide], values["d"][:, 2 * wide:]
    move("fa", "ua", y_up)
    move("fb", "db", y_down)

    gate("u2", "d2", "u", "d", "n")
    move("u3", "u2", z_up)
    move("d3", "d2", z_down)

    gate("fa", "fb", "u2", "d2", "n")
    move("nu", "n", y_up)
    move("nd", "n", y_down)
    move("nfa", "fa", x_side)
    move("nfb", "fb", x_side)

    gate("u3", "d3")
    values["u3h"], values["d3h"] = values["u3"][:rows], values["d3"][rows:]
    move("u4", "u3h", z_up)
    move("d4", "d3h", z_down)

    a_pieces = [("p", 0, 0), ("u1", 0, Z - 1), ("d1", 0, 1), ("u2", 0, Z - 2), ("d2", 0, 2),
                ("u3", 0, Z - 3), ("d3", 0, 3), ("u4", 0, Z // 2), ("d4", 1, Z // 2)]
    gate("nfa", "u4")
    left = packed_left([(values[k], tuple(v)) for k, *v in a_pieces], rows)
    pieces, sizes, came = {}, {}, {}
    for chunk, first in (("b", 2 * wide), ("a", 0)):
        names = [("o", 0, 0, first), ("n", 1, 0, first), ("u", 0, Y - 1, first), ("d", 0, 1, first), ("f" + chunk, 0, 2, 0),
                 ("nu", 1, Y - 1, first), ("nd", 1, 1, first), ("nf" + chunk, 1, 2, 0)]
        pieces[chunk] = [(values[k], tuple(v)) for k, *v in names]
        sizes[chunk] = values["f" + chunk].shape[1]
        send = product(left, pieces[chunk], sizes[chunk], 1)
        came[chunk] = moved(send, sibling)
        left, _ = lax.optimization_barrier((left, send))
    parts = []
    for chunk in "ba":
        keep = product(left, pieces[chunk], sizes[chunk], 0)
        away = (keep[1] + came[chunk][1].astype(jnp.float32)).astype(jnp.bfloat16)
        arrived = moved(away, x_pair)
        left, _ = lax.optimization_barrier((left, away))
        parts.append((keep[0] + came[chunk][0].astype(jnp.float32) + arrived.astype(jnp.float32)).astype(jnp.bfloat16))
    first = lax.pad(parts[0], jnp.zeros((), jnp.bfloat16), ((0, 0, 0), (wide, 0, 0)))
    return lax.dynamic_update_slice(first, parts[1], (0, 0))


def solution(mesh):
    in_specs = (P("col", "row"), P("col", "row"))
    out_specs = P("col", ("row", "depth"))
    return jax.shard_map(body, mesh=mesh, in_specs=in_specs, out_specs=out_specs, check_vma=False)
```

```python
import functools

import jax
import jax.numpy as jnp
from jax import lax
from jax.experimental import pallas as pl
from jax.experimental.pallas import tpu as pltpu
from jax.sharding import PartitionSpec as P

AXES = ("row", "col", "depth")
Z, X, Y = 8, 2, 4
TILE = 256


def moved(value, target):
    def number(z, x_hi, y, core, x_lo):
        return (((z * X + x_hi) * Y + y) * 2 + core) * 2 + x_lo

    pairs = [
        (number(z, x_hi, y, core, x_lo), number(*target(z, x_hi, y, core, x_lo)))
        for z in range(Z)
        for x_hi in range(X)
        for y in range(Y)
        for core in range(2)
        for x_lo in range(2)
    ]
    return lax.ppermute(value, AXES, pairs)


def z_up(z, x_hi, y, core, x_lo):
    return (z + 1) % Z, x_hi, y, core, x_lo


def z_down(z, x_hi, y, core, x_lo):
    return (z - 1) % Z, x_hi, y, core, x_lo


def y_up(z, x_hi, y, core, x_lo):
    return z, x_hi, (y + 1) % Y, core, x_lo


def y_down(z, x_hi, y, core, x_lo):
    return z, x_hi, (y - 1) % Y, core, x_lo


def x_side(z, x_hi, y, core, x_lo):
    return z, 1 - x_hi, y, core, 1 - x_lo


def x_pair(z, x_hi, y, core, x_lo):
    return z, x_hi, y, core, 1 - x_lo


def sibling(z, x_hi, y, core, x_lo):
    return z, x_hi, y, 1 - core, x_lo


def pack_kernel(places, *refs):
    pieces, packed, sem = refs[:len(places)], refs[-2], refs[-1]
    rows = packed.shape[1] // 2
    z = lax.axis_index("row")
    copies = []
    for index, (block, offset) in enumerate(places):
        place = packed.at[lax.rem(z + offset, Z), pl.ds(block * rows, pieces[index].shape[0])]
        copies.append(pltpu.make_async_copy(pieces[index], place, sem.at[index]))
    for copy in copies:
        copy.start()
    for copy in copies:
        copy.wait()


def packed_left(pieces, rows):
    values, places = zip(*pieces)
    half = values[0].shape[1]
    return pl.pallas_call(
        functools.partial(pack_kernel, places),
        out_shape=jax.ShapeDtypeStruct((Z, 2 * rows, half), jnp.bfloat16),
        in_specs=[pl.BlockSpec(memory_space=pl.ANY)] * len(values),
        out_specs=pl.BlockSpec(memory_space=pltpu.VMEM),
        scratch_shapes=[pltpu.SemaphoreType.DMA((len(values),))],
        compiler_params=pltpu.CompilerParams(vmem_limit_bytes=12 * 1024 * 1024),
        cost_estimate=pl.CostEstimate(flops=0, bytes_accessed=8 * Z * rows * half, transcendentals=0),
    )(*values)


def product_kernel(places, block, left, *refs):
    rights = refs[:len(places)]
    target, total = refs[len(places):]
    _, rows, share = target.shape
    col = lax.axis_index("col")
    x_lo = lax.axis_index("depth")
    x_hi, y = col // (2 * Y), col // 2 % Y
    for index, (side, dy, first, start, width) in enumerate(places):
        place = lax.rem(x_hi + side, X) * Y + lax.rem(y + dy, Y)
        term = jnp.dot(
            left[place, block * rows:(block + 1) * rows],
            rights[index][:, first:first + width],
            preferred_element_type=jnp.float32,
        )
        here = slice(start, start + width)
        total[:, here] = total[:, here] + term if index else term
    for d in range(2):
        target[lax.rem(x_lo + d, 2)] = total[:, d * share:(d + 1) * share].astype(target.dtype)


def product(left, pieces, columns, block):
    values, places = zip(*pieces)
    rows, inner = left.shape[1] // 2, left.shape[0] * left.shape[2]
    vmem = pl.BlockSpec(memory_space=pltpu.VMEM)
    return pl.pallas_call(
        functools.partial(product_kernel, places, block),
        out_shape=jax.ShapeDtypeStruct((2, rows, columns // 2), jnp.bfloat16 if block else jnp.float32),
        in_specs=[vmem] * (1 + len(values)),
        out_specs=vmem,
        scratch_shapes=[pltpu.VMEM((rows, columns), jnp.float32)],
        compiler_params=pltpu.CompilerParams(vmem_limit_bytes=24 * 1024 * 1024),
        cost_estimate=pl.CostEstimate(
            flops=2 * rows * inner * columns, bytes_accessed=2 * inner * (rows + columns), transcendentals=0
        ),
    )(left, *values)


class Held:
    def __init__(self, **values):
        self.values = dict(values)

    def gate(self, *names):
        names = list(dict.fromkeys(names))
        if len(names) > 1:
            for name, value in zip(names, lax.optimization_barrier([self.values[n] for n in names]), strict=True):
                self.values[name] = value

    def move(self, name, source, target, after=()):
        self.gate(source, *after)
        self.values[name] = moved(self.values[source], target)


def body(a_matrix, b_matrix):
    rows = a_matrix.shape[0]
    depth, columns = b_matrix.shape
    half = depth // 2
    share = columns // 2
    col = lax.axis_index("col")
    x_lo = lax.axis_index("depth")
    x_hi, core = col // (2 * Y), col % 2
    part = x_hi ^ x_lo
    split = -(-share // (2 * TILE)) * 2 * TILE
    wide = share - TILE

    def cut(first, width):
        return jnp.concatenate(
            [lax.dynamic_slice(b_matrix, (part * half, d * share + first), (half, width)) for d in range(2)], 1
        )

    other = lax.dynamic_slice(a_matrix, (0, (1 - core) * depth + part * half), (rows, half))
    mine = lax.dynamic_slice(a_matrix, (0, core * depth + part * half), (rows, half))
    held = Held(o=jnp.concatenate([cut(0, wide), cut(wide, share - wide)], 1))
    values, move, gate = held.values, held.move, held.gate
    values["other"] = other
    move("sib", "other", sibling)
    gate("sib", "o")
    move("u", "o", y_up)
    move("d", "o", y_down)
    move("n", "o", x_side)
    values["p"] = jnp.concatenate([mine, values["sib"]], 0)
    move("u1", "p", z_up)
    move("d1", "p", z_down)

    gate("u1", "d1")
    move("u2", "u1", z_up)
    move("d2", "d1", z_down)

    gate("u", "d", "n")
    values["ua"], values["db"] = values["u"][:, :split], values["d"][:, split:]
    move("fa", "ua", y_up)
    move("fb", "db", y_down)

    gate("u2", "d2", "u", "d", "n")
    move("u3", "u2", z_up)
    move("d3", "d2", z_down)

    gate("fa", "fb", "u2", "d2", "n")
    move("nu", "n", y_up)
    move("nd", "n", y_down)
    move("nfa", "fa", x_side)
    move("nfb", "fb", x_side)

    gate("u3", "d3")
    values["u3h"], values["d3h"] = values["u3"][:rows], values["d3"][rows:]
    move("u4", "u3h", z_up)
    move("d4", "d3h", z_down)

    a_pieces = [("p", 0, 0), ("u1", 0, Z - 1), ("d1", 0, 1), ("u2", 0, Z - 2), ("d2", 0, 2),
                ("u3", 0, Z - 3), ("d3", 0, 3), ("u4", 0, Z // 2), ("d4", 1, Z // 2)]
    gate("nfa", "u4")
    left = packed_left([(values[k], tuple(v)) for k, *v in a_pieces], rows)
    pieces, sizes, came = {}, {}, {}
    for chunk, first, size in (("b", 2 * wide, columns - 2 * wide), ("a", 0, 2 * wide)):
        names = []
        for name, side, dy in (("o", 0, 0), ("n", 1, 0), ("u", 0, Y - 1), ("d", 0, 1), ("nu", 1, Y - 1), ("nd", 1, 1)):
            names.append((name, side, dy, first, 0, size))
        for name, side in (("f", 0), ("nf", 1)):
            if first < split:
                names.append((name + "a", side, 2, first, 0, min(size, split - first)))
            if first + size > split:
                start = max(split - first, 0)
                names.append((name + "b", side, 2, first + start - split, start, size - start))
        pieces[chunk] = [(values[k], tuple(v)) for k, *v in names]
        sizes[chunk] = size
        send = product(left, pieces[chunk], sizes[chunk], 1)
        if came:
            send, came["b"] = lax.optimization_barrier((send, came["b"]))
        came[chunk] = moved(send, sibling)
        left, _ = lax.optimization_barrier((left, send))
    parts = []
    for chunk in "ba":
        keep = product(left, pieces[chunk], sizes[chunk], 0)
        away = (keep[1] + came[chunk][1].astype(jnp.float32)).astype(jnp.bfloat16)
        if parts:
            away, before = lax.optimization_barrier((away, before))
        arrived = moved(away, x_pair)
        before = arrived
        left, _ = lax.optimization_barrier((left, away))
        parts.append((keep[0] + came[chunk][0].astype(jnp.float32) + arrived.astype(jnp.float32)).astype(jnp.bfloat16))
    first = lax.pad(parts[0], jnp.zeros((), jnp.bfloat16), ((0, 0, 0), (wide, 0, 0)))
    return lax.dynamic_update_slice(first, parts[1], (0, 0))


def solution(mesh):
    in_specs = (P("col", "row"), P("col", "row"))
    out_specs = P("col", ("row", "depth"))
    return jax.shard_map(body, mesh=mesh, in_specs=in_specs, out_specs=out_specs, check_vma=False)
```
